32 devices in a mesh: track: 8 (over y, x, core), width: 4 (over z).
Axes of the slice: x: 2, y: 2, z: 4, core: 2. Of those that a mesh axis runs over, the one named last changes fastest.
Arguments:
- phase: float32 [256, 256, 512], P('track', 'width'), may hold values from -1 to 1
- solute: float32 [256, 256, 512], P('track', 'width'), may hold values from -0.5 to 0.5
- heat_rows: float32 [2048, 512], P(('track', 'width')), may hold values from -4 to 4
- rate_rows: float32 [2048, 512], P(('track', 'width')), may hold values from -6 to 6
- dest_tile: int32 [2048, 1], P(('track', 'width')), may hold values from 0 to 31; in each aligned block of 64 rows (0 to 63, 64 to 127, ...) at most 4 rows name the same one
- dest_block: int32 [2048], P(('track', 'width')), may hold values from 0 to 31
- active: int32 [32, 32], P('track', 'width'), may hold values 0 or 1
Outputs:
- phase_out: float32 [256, 256, 512], P('track', 'width')
- solute_out: float32 [256, 256, 512], P('track', 'width')
The draws below stay inside these ranges and needn't reach their ends.
Inputs may be any that keep to these rules, and one draw needn't show every extreme that they name: `dest_tile`: the rows of one device send at most 4 rows to one tile, and exactly 4 to some tile.
All inputs are finite; a program needn't handle non-finite values. No bound on the sum of `active` on one device may be relied on, other than what follows from the above.
Results may differ from the reference program's by a relative error of at most 0.0003.
Values sent between devices are 32-bit elements; how exact they have to be, the bound alone decides.
A program may use at most 128 MiB of HBM per device.

```python
import math
import jax
import jax.numpy as jnp
import numpy as np

CX = 32
CY = 64
CZ = 512
BS = 8
STEPS = 3
CAP = 4
ROWS_DEV = 64
ROWS = 2048
NX = 256
NY = 256
NZ = 512
NBX = 32
NBY = 32
TILE_BLOCKS = 32
DEVICES = 32


def touch_ends(values, stream_key, least, top_value):
    longest = values.shape.index(max(values.shape))
    spots = []
    for shift in (0, 1):
        where = [jax.random.randint(jax.random.fold_in(stream_key, axis), (), 0, length) for axis, length in enumerate(values.shape)]
        where[longest] = (where[longest] + shift) % values.shape[longest]
        spots.append(tuple(where))
    return values.at[spots[0]].set(least).at[spots[1]].set(top_value)


def steps_of(key, dims, split, smallest, high):
    def one(dim, shards_of):
        heights = jax.random.uniform(jax.random.fold_in(jax.random.fold_in(key, 6), dim), (shards_of,), jnp.float32, smallest / len(split), high / len(split))
        return jnp.repeat(jnp.exp(heights), dims[dim] // shards_of).reshape((-1,) + (1,) * (len(dims) - dim - 1))

    factor_of = one(*split[0])
    for cut in split[1:]:
        factor_of = factor_of * one(*cut)
    return factor_of


def shared_out(stream_key, own, number, rows, amount, top, reach, slope):
    sequence = jax.random.permutation(stream_key, amount)
    crowded, ordinary = shares(amount, rows * top, reach, slope, True), shares(amount, rows * top, reach, slope, False)
    places = jnp.arange(amount)

    def named(sizes, turn):
        used = int((sizes > 0).sum())
        fixed = max(1, used // 4)
        moved = fixed + (places - fixed + turn * (used - fixed)) % max(1, amount - fixed)
        return jnp.zeros((amount,), jnp.int32).at[sequence[jnp.where(places < fixed, places, moved)]].set(jnp.asarray(sizes, jnp.int32))

    sizes = jnp.where(number % 4 == 0, named(crowded, number // 4), named(ordinary, number - number // 4 - 1))
    mixed = jax.random.permutation(jax.random.fold_in(own, 3), amount)
    donor, sink = mixed[0:amount // 2 * 2:2], mixed[1:amount // 2 * 2:2]
    room = jnp.minimum(sizes[donor] - 1, reach - sizes[sink]) // 2
    room = jnp.where((donor == sequence[0]) | (sink == sequence[0]) | (sizes[sink] == 0), 0, jnp.maximum(room, 0))
    moved = jax.random.randint(jax.random.fold_in(own, 4), (amount // 2,), 0, 1 << 20) % (room + 1)
    sizes = sizes.at[donor].add(-moved).at[sink].add(moved)
    labels = jnp.searchsorted(jnp.cumsum(sizes), jnp.arange(rows * top), side="right").astype(jnp.int32)
    table = labels.reshape(top, rows).T
    table = table[jax.random.permutation(jax.random.fold_in(own, 1), rows)]
    turn = jax.random.randint(jax.random.fold_in(own, 2), (rows, 1), 0, top)
    return jnp.take_along_axis(table, (jnp.arange(top)[None, :] + turn) % top, axis=1)


def shares(count, total, most, slope, full):
    loads = [(1 << 20) // math.isqrt(standing ** slope) + 1 for standing in range(1, count + 1)]
    largest = most if full else min(most, max(-(-total // count), total * loads[0] // sum(loads)))
    least = 1 if total - largest >= count - 1 else 0
    holding, surplus = [largest] + [least] * (count - 1), total - largest - least * (count - 1)
    while surplus > 0:
        candidates = [i for i in range(1, count) if holding[i] < largest] or [i for i in range(1, count) if holding[i] < most]
        whole, remaining = sum([loads[i] for i in candidates]), surplus
        for i in candidates:
            extra = min(most - holding[i], max(1, remaining * loads[i] // whole), surplus)
            holding[i] = holding[i] + extra
            surplus = surplus - extra
    return np.array(holding)


def bell_draw(rng, shape, width, most, cuts=(), dtype=jnp.bfloat16):
    drawn = jax.random.normal(rng, shape, jnp.float32) * width
    if len(cuts) > 0:
        drawn = steps_of(rng, shape, cuts, -0.22, 0.18) * drawn
    return jnp.clip(drawn, min=-most, max=most).astype(dtype)


def setup_inputs(seed: int = 0) -> dict:
    splits = jax.random.split(jax.random.key(seed), 8)
    phase = jnp.clip(jax.random.uniform(splits[0], (NX, NY, NZ), jnp.float32, -1.0, 1.0) * steps_of(splits[0], (NX, NY, NZ), ((0, 8), (1, 4)), -0.4, 0.0), -1.0, 1.0)
    solute = jnp.clip(jax.random.uniform(splits[1], (NX, NY, NZ), jnp.float32, -0.5, 0.5) * steps_of(splits[1], (NX, NY, NZ), ((0, 8), (1, 4)), -0.4, 0.0), -0.5, 0.5)
    heat_rows = bell_draw(splits[2], (ROWS, CZ), 0.3, 4.0, ((0, 32),), jnp.float32)
    rate_rows = bell_draw(splits[3], (ROWS, CZ), 0.6, 6.0, ((0, 32),), jnp.float32)
    dest_tile_keys = jax.random.split(jax.random.fold_in(splits[4], 1), ROWS // ROWS_DEV)
    dest_tile_turns = jax.random.permutation(jax.random.fold_in(splits[4], 3), ROWS // ROWS_DEV)
    dest_tile = jax.vmap(lambda own, number: shared_out(jax.random.fold_in(splits[4], 2), own, number, ROWS_DEV, DEVICES, 1, CAP, 2))(dest_tile_keys, dest_tile_turns).reshape((ROWS, 1))
    dest_block = touch_ends(jax.random.randint(splits[5], (ROWS,), 0, TILE_BLOCKS), jax.random.fold_in(splits[5], 1), 0, TILE_BLOCKS - 1).astype(jnp.int32)
    active = touch_ends((jax.random.randint(splits[6], (NBX, NBY), 0, 5) < 3).astype(jnp.int32), jax.random.fold_in(splits[6], 1), 0, 1)
    return dict(phase=phase, solute=solute, heat_rows=heat_rows, rate_rows=rate_rows, dest_tile=dest_tile, dest_block=dest_block, active=active)


coef_track = 0.9
coef_width = 0.6
coef_depth = 0.35
time_step = 0.1
coupling = 1.6
diffusion = 0.8


def laplace(padded, along_first, along_second, along_third):
    depth_pad = jnp.pad(padded, ((0, 0), (0, 0), (1, 1)))
    center = padded[1:-1, 1:-1, :]
    first = padded[2:, 1:-1, :] + padded[:-2, 1:-1, :] - 2.0 * center
    second = padded[1:-1, 2:, :] + padded[1:-1, :-2, :] - 2.0 * center
    third = depth_pad[1:-1, 1:-1, 2:] + depth_pad[1:-1, 1:-1, :-2] - 2.0 * center
    return along_first * first + along_second * second + along_third * third


def advance(phase_ext, solute_ext, heat, rate, cells, count):
    inner_phase = phase_ext[1:-1, 1:-1, :]
    inner_solute = solute_ext[1:-1, 1:-1, :]
    theta = heat - (count * time_step) * rate
    bond = 1.0 - inner_phase * inner_phase
    drive = laplace(phase_ext, coef_track, coef_width, coef_depth) + inner_phase - inner_phase * inner_phase * inner_phase - coupling * bond * bond * (theta + inner_solute)
    change = cells * drive
    new_phase = inner_phase + time_step * change
    new_solute = inner_solute + time_step * (diffusion * laplace(solute_ext, 1.0, 1.0, 1.0) + 0.5 * change)
    return new_phase, new_solute


def expand(blocks, size):
    return jnp.repeat(jnp.repeat(blocks, size, axis=0), size, axis=1)


def reference(phase, solute, heat_rows, rate_rows, dest_tile, dest_block, active):
    blocks_x = CX // BS
    blocks_y = CY // BS
    tiles_across = NY // CY
    tile = dest_tile[:, 0].astype(jnp.int32)
    track_pos = tile // tiles_across
    width_pos = tile % tiles_across
    global_x = track_pos * blocks_x + dest_block // blocks_y
    global_y = width_pos * blocks_y + dest_block % blocks_y
    segment = (global_x * NBY + global_y).astype(jnp.int32)
    heat_blocks = jax.ops.segment_sum(heat_rows, segment, num_segments=NBX * NBY).reshape(NBX, NBY, NZ)
    rate_blocks = jax.ops.segment_sum(rate_rows, segment, num_segments=NBX * NBY).reshape(NBX, NBY, NZ)
    heat = expand(heat_blocks, BS)
    rate = expand(rate_blocks, BS)
    cells = expand(active.astype(jnp.float32), BS)[:, :, None]
    edges = ((1, 1), (1, 1), (0, 0))
    for count in range(STEPS):
        phase, solute = advance(jnp.pad(phase, edges), jnp.pad(solute, edges), heat, rate, cells, count)
    return phase, solute
```

```python
import functools

import jax
import jax.numpy as jnp
from jax import lax
from jax.experimental import pallas as pl
from jax.experimental.pallas import tpu as pltpu
from jax.sharding import PartitionSpec as P

BS = 8
CAP = 4
STEPS = 3
LANES = 128
PAD = 8
MESH = pl.DeviceIdType.MESH
HIGH = lax.Precision.HIGHEST

coef_track = 0.9
coef_width = 0.6
coef_depth = 0.35
time_step = 0.1
coupling = 1.6
diffusion = 0.8
center_phase = 1.0 - 2.0 * (coef_track + coef_width + coef_depth)
center_solute = 1.0 - 6.0 * time_step * diffusion


def track_kernel(sizes, phase, solute, heat_rows, rate_rows, dest_tile, dest_block, active,
                 phase_out, solute_out,
                 f0, f1, y_send, y_recv, label_out, label_in, heat_out, heat_in, rate_out, rate_in,
                 selector, theta,
                 load_sem, store_sem, x_send_sem, x_recv_sem, y_send_sem, y_recv_sem,
                 label_sems, heat_sems, rate_sems):
    tracks, widths, nx, ny, nz, rows = sizes
    devices = tracks * widths
    zt_n = nz // LANES
    pairs = zt_n // 2
    bx_n = nx // BS
    by_n = ny // BS
    t = lax.axis_index("track")
    w = lax.axis_index("width")
    me = t * widths + w

    def loads():
        out = []
        for f, ref in enumerate((phase, solute)):
            for zt in range(zt_n):
                out.append(pltpu.make_async_copy(
                    ref.at[:, :, pl.ds(zt * LANES, LANES)],
                    f0.at[f, pl.ds(1, nx), zt, pl.ds(PAD, ny), :],
                    load_sem.at[f, zt]))
        return out

    for copy in loads():
        copy.start()

    barrier = pltpu.get_barrier_semaphore()

    def where(k):
        to = lax.rem(me + k, devices)
        return {"track": to // widths, "width": lax.rem(to, widths)}

    def greet(k, carry):
        pl.semaphore_signal(barrier, inc=1, device_id=where(k), device_id_type=MESH)
        return carry

    lax.fori_loop(1, devices, greet, 0)

    tcol = dest_tile[...].astype(jnp.float32)
    eye = lax.broadcasted_iota(jnp.int32, (rows, rows), 0) == lax.broadcasted_iota(jnp.int32, (rows, rows), 1)
    trow = jnp.sum(jnp.where(eye, tcol, 0.0), axis=0, keepdims=True)
    before = lax.broadcasted_iota(jnp.int32, (rows, rows), 0) < lax.broadcasted_iota(jnp.int32, (rows, rows), 1)
    rank = jnp.sum(jnp.where(before & (tcol == trow), 1.0, 0.0), axis=0, keepdims=True)
    slot = trow * CAP + rank
    index = lax.broadcasted_iota(jnp.int32, (8 * devices, rows), 0)
    slot_of = ((index >> 3) * CAP + (index & 3)).astype(jnp.float32)
    pick = jnp.where(slot_of == slot, 1.0, 0.0)
    labels = dest_block[...].astype(jnp.float32) + 1.0
    label_col = jnp.sum(pick * labels, axis=1, keepdims=True).reshape(devices, 8, 1)
    diagonal = lax.broadcasted_iota(jnp.int32, (devices, 8, LANES), 1) == lax.broadcasted_iota(
        jnp.int32, (devices, 8, LANES), 2)
    label_out[...] = jnp.sum(jnp.where(diagonal, label_col, 0.0), axis=1, keepdims=True)
    low = lax.broadcasted_iota(jnp.int32, (8 * devices, LANES), 0) & 7 < 4

    def pack_rows(source, target):
        moved = jnp.dot(pick, source[...], precision=HIGH, preferred_element_type=jnp.float32)
        for j in range(pairs):
            first = moved[:, 2 * j * LANES:(2 * j + 1) * LANES]
            second = moved[:, (2 * j + 1) * LANES:(2 * j + 2) * LANES]
            target[:, j] = jnp.where(low, first, second).reshape(devices, 8, LANES)

    pack_rows(heat_rows, heat_out)
    pack_rows(rate_rows, rate_out)

    has = (t > 0, t < tracks - 1, w > 0, w < widths - 1)
    for side in range(2):
        @pl.when(jnp.logical_not(has[side]))
        def _():
            edge = jnp.zeros((2, zt_n, ny, LANES), jnp.float32)
            f0[:, side * (nx + 1), :, pl.ds(PAD, ny), :] = edge
            f1[:, side * (nx + 1), :, pl.ds(PAD, ny), :] = edge

        @pl.when(jnp.logical_not(has[2 + side]))
        def _():
            y_recv[:, side] = jnp.zeros((STEPS, 2, nx, zt_n, 1, LANES), jnp.float32)

    pl.semaphore_wait(barrier, devices - 1)

    def exchange(source, target, sems, k):
        return pltpu.make_async_remote_copy(
            src_ref=source.at[lax.rem(me + k, devices)], dst_ref=target.at[me],
            send_sem=sems.at[0, k], recv_sem=sems.at[1, k],
            device_id=where(k), device_id_type=MESH)

    def own(source, target, sems):
        return pltpu.make_async_copy(source.at[me], target.at[me], sems.at[0, 0])

    def send_all(*triples):
        for triple in triples:
            own(*triple).start()

        def body(k, carry):
            for triple in triples:
                exchange(*triple, k).start()
            return carry

        lax.fori_loop(1, devices, body, 0)

    def wait_all(*triples):
        for triple in triples:
            own(*triple).wait()

        def body(k, carry):
            for triple in triples:
                exchange(*triple, k).wait()
            return carry

        lax.fori_loop(1, devices, body, 0)

    labels_x = (label_out, label_in, label_sems)
    heat_x = (heat_out, heat_in, heat_sems)
    rate_x = (rate_out, rate_in, rate_sems)
    send_all(labels_x, heat_x)

    def x_copy(field, stage, side):
        return pltpu.make_async_remote_copy(
            src_ref=field.at[:, 1 if side == 0 else nx, :, pl.ds(PAD, ny), :],
            dst_ref=field.at[:, nx + 1 if side == 0 else 0, :, pl.ds(PAD, ny), :],
            send_sem=x_send_sem.at[stage, side], recv_sem=x_recv_sem.at[stage, side],
            device_id={"track": t + (2 * side - 1)}, device_id_type=MESH)

    def y_copy(stage, side):
        return pltpu.make_async_remote_copy(
            src_ref=y_send.at[stage, side], dst_ref=y_recv.at[stage, 1 - side],
            send_sem=y_send_sem.at[stage, side], recv_sem=y_recv_sem.at[stage, side],
            device_id={"width": w + (2 * side - 1)}, device_id_type=MESH)

    def send_halo(field, stage):
        for side in range(2):
            @pl.when(has[side])
            def _():
                x_copy(field, stage, side).start()

        def pack(x, carry):
            for side, row in ((0, PAD), (1, PAD + ny - 1)):
                for f in range(2):
                    for zt in range(zt_n):
                        y_send[stage, side, f, x, zt] = field[f, x + 1, zt, pl.ds(row, 1), :]
            return carry

        lax.fori_loop(0, nx, pack, 0)
        for side in range(2):
            @pl.when(has[2 + side])
            def _():
                y_copy(stage, side).start()

    def wait_halo(field, stage):
        for side in range(2):
            @pl.when(has[side])
            def _():
                x_copy(field, stage, side).wait_send()
                x_copy(field, stage, 1 - side).wait_recv()

            @pl.when(has[2 + side])
            def _():
                y_copy(stage, side).wait_send()
                y_copy(stage, 1 - side).wait_recv()

        def unpack(x, carry):
            for side, row in ((0, PAD - 1), (1, PAD + ny)):
                for f in range(2):
                    for zt in range(zt_n):
                        field[f, x + 1, zt, pl.ds(row, 1), :] = y_recv[stage, side, f, x, zt]
            return carry

        lax.fori_loop(0, nx, unpack, 0)

    lane = lax.broadcasted_iota(jnp.int32, (BS, LANES), 1)
    first_lane = lane == 0
    last_lane = lane == LANES - 1

    def depth_sum(tiles):
        up = [pltpu.roll(v, 1, 1) for v in tiles]
        down = [pltpu.roll(v, LANES - 1, 1) for v in tiles]
        sums = []
        for zt in range(zt_n):
            below = jnp.where(first_lane, up[zt - 1] if zt > 0 else 0.0, up[zt])
            above = jnp.where(last_lane, down[zt + 1] if zt < zt_n - 1 else 0.0, down[zt])
            sums.append(below + above)
        return sums

    def cell_block(src, dst, count, x, by):
        bx = x >> 3
        rate_of = active[bx, by].astype(jnp.float32) * time_step
        here = pl.ds(PAD + BS * by, BS)
        back = pl.ds(PAD + BS * by - 1, BS)
        ahead = pl.ds(PAD + BS * by + 1, BS)
        p = [src[0, x + 1, zt, here, :] for zt in range(zt_n)]
        s = [src[1, x + 1, zt, here, :] for zt in range(zt_n)]
        pz = depth_sum(p)
        sz = depth_sum(s)
        for zt in range(zt_n):
            px = src[0, x, zt, here, :] + src[0, x + 2, zt, here, :]
            py = src[0, x + 1, zt, back, :] + src[0, x + 1, zt, ahead, :]
            sx = src[1, x, zt, here, :] + src[1, x + 2, zt, here, :]
            sy = src[1, x + 1, zt, back, :] + src[1, x + 1, zt, ahead, :]
            square = p[zt] * p[zt]
            bond = 1.0 - square
            drive = coef_track * px + coef_width * py + coef_depth * pz[zt] + p[zt] * (center_phase - square)
            sink = s[zt] if count == 0 else s[zt] + theta[count - 1, bx, zt, by:by + 1, :]
            drive = drive - coupling * bond * bond * sink
            change = rate_of * drive
            dst[0, x + 1, zt, here, :] = p[zt] + change
            dst[1, x + 1, zt, here, :] = (
                center_solute * s[zt] + (time_step * diffusion) * (sx + sy + sz[zt]) + 0.5 * change)

    def heat_block(src, dst, x, by):
        bx = x >> 3
        rate_of = active[bx, by].astype(jnp.float32) * (time_step * coupling)
        here = pl.ds(PAD + BS * by, BS)
        for zt in range(zt_n):
            p = src[0, x + 1, zt, here, :]
            bond = 1.0 - p * p
            change = bond * bond * (rate_of * theta[0, bx, zt, by:by + 1, :])
            dst[0, x + 1, zt, here, :] = dst[0, x + 1, zt, here, :] - change
            dst[1, x + 1, zt, here, :] = dst[1, x + 1, zt, here, :] - 0.5 * change

    def sweep(block, xs, bys):
        low_x, high_x, stride = xs

        def body(i, carry):
            for by in bys:
                block(low_x + stride * i, by)
            return carry

        lax.fori_loop(0, (high_x - low_x + stride - 1) // stride, body, 0)

    inner = range(1, by_n - 1)
    outer = (0, by_n - 1)

    def boundary(block):
        sweep(block, (0, nx, nx - 1), range(by_n))
        sweep(block, (1, nx - 1, 1), outer)

    def arrived(rows_in):
        both = jnp.concatenate([rows_in[:, j].reshape(8 * devices, LANES) for j in range(pairs)], axis=1)
        return lax.dot_general(selector[...], both, (((0,), (0,)), ((), ())), precision=HIGH,
                               preferred_element_type=jnp.float32)

    def tile_of(summed, bx, zt):
        at = (zt % 2) * (LANES // 2) + bx * by_n
        return summed[at:at + by_n, (zt // 2) * LANES:(zt // 2 + 1) * LANES]

    for copy in loads():
        copy.wait()
    send_halo(f0, 0)
    send_all(rate_x)

    step0 = functools.partial(cell_block, f0, f1, 0)
    step1 = functools.partial(cell_block, f1, f0, 1)
    step2 = functools.partial(cell_block, f0, f1, 2)
    finish = functools.partial(heat_block, f0, f1)

    sweep(step0, (1, nx - 1, 1), inner)
    wait_halo(f0, 0)
    boundary(step0)

    wait_all(labels_x, heat_x)
    spread = jnp.where(diagonal, jnp.broadcast_to(label_in[...], (devices, 8, LANES)), 0.0)
    label_in_col = jnp.sum(spread, axis=2, keepdims=True) - 1.0
    place = lax.broadcasted_iota(jnp.int32, (devices, 8, LANES), 2) - (LANES // 2) * (
        lax.broadcasted_iota(jnp.int32, (devices, 8, LANES), 1) >> 2)
    selector[...] = jnp.where(place.astype(jnp.float32) == label_in_col, 1.0, 0.0).reshape(8 * devices, LANES)
    heat = arrived(heat_in)
    for bx in range(bx_n):
        for zt in range(zt_n):
            theta[0, bx, zt] = tile_of(heat, bx, zt)

    boundary(finish)
    send_halo(f1, 1)
    sweep(finish, (1, nx - 1, 1), inner)

    wait_all(rate_x)
    rate = arrived(rate_in)
    for bx in range(bx_n):
        for zt in range(zt_n):
            whole = theta[0, bx, zt]
            slope = tile_of(rate, bx, zt)
            theta[0, bx, zt] = whole - time_step * slope
            theta[1, bx, zt] = whole - (2 * time_step) * slope

    half = nx // 2
    sweep(step1, (1, half, 1), inner)
    wait_halo(f1, 1)
    boundary(step1)
    send_halo(f0, 2)
    sweep(step1, (half, nx - 1, 1), inner)
    sweep(step2, (1, nx - 1, 1), inner)

    def stores(part, x_at, x_len, y_at, y_len):
        out = []
        for f, ref in enumerate((phase_out, solute_out)):
            for zt in range(zt_n):
                out.append(pltpu.make_async_copy(
                    f1.at[f, pl.ds(1 + x_at, x_len), zt, pl.ds(PAD + y_at, y_len), :],
                    ref.at[pl.ds(x_at, x_len), pl.ds(y_at, y_len), pl.ds(zt * LANES, LANES)],
                    store_sem.at[part, f, zt]))
        return out

    middle = stores(0, 1, nx - 2, BS, ny - 2 * BS)
    for copy in middle:
        copy.start()
    wait_halo(f0, 2)
    boundary(step2)
    rim = (stores(1, 0, 1, 0, ny) + stores(2, nx - 1, 1, 0, ny)
           + stores(3, 1, nx - 2, 0, BS) + stores(4, 1, nx - 2, ny - BS, BS))
    for copy in rim:
        copy.start()
    for copy in middle + rim:
        copy.wait()


def solution(mesh):
    tracks = mesh.shape["track"]
    widths = mesh.shape["width"]
    devices = tracks * widths

    def on_device(phase, solute, heat_rows, rate_rows, dest_tile, dest_block, active):
        nx, ny, nz = phase.shape
        rows = heat_rows.shape[0]
        zt_n = nz // LANES
        pairs = zt_n // 2
        f32 = jnp.float32
        field = pltpu.VMEM((2, nx + 2, zt_n, ny + 2 * PAD, LANES), f32)
        ends = pltpu.VMEM((STEPS, 2, 2, nx, zt_n, 1, LANES), f32)
        label = pltpu.VMEM((devices, 1, LANES), f32)
        moved = pltpu.VMEM((devices, pairs, 8, LANES), f32)
        vmem = pl.BlockSpec(memory_space=pltpu.VMEM)
        any_space = pl.BlockSpec(memory_space=pl.ANY)
        return pl.pallas_call(
            functools.partial(track_kernel, (tracks, widths, nx, ny, nz, rows)),
            out_shape=(jax.ShapeDtypeStruct(phase.shape, f32), jax.ShapeDtypeStruct(solute.shape, f32)),
            in_specs=[any_space, any_space, vmem, vmem, vmem, vmem,
                      pl.BlockSpec(memory_space=pltpu.SMEM)],
            out_specs=(any_space, any_space),
            scratch_shapes=[
                field, field, ends, ends, label, label, moved, moved, moved, moved,
                pltpu.VMEM((8 * devices, LANES), f32),
                pltpu.VMEM((2, nx // BS, zt_n, ny // BS, LANES), f32),
                pltpu.SemaphoreType.DMA((2, zt_n)),
                pltpu.SemaphoreType.DMA((5, 2, zt_n)),
                pltpu.SemaphoreType.DMA((STEPS, 2)),
                pltpu.SemaphoreType.DMA((STEPS, 2)),
                pltpu.SemaphoreType.DMA((STEPS, 2)),
                pltpu.SemaphoreType.DMA((STEPS, 2)),
                pltpu.SemaphoreType.DMA((2, devices)),
                pltpu.SemaphoreType.DMA((2, devices)),
                pltpu.SemaphoreType.DMA((2, devices)),
            ],
            compiler_params=pltpu.CompilerParams(
                collective_id=0, has_side_effects=True, vmem_limit_bytes=56 * 1024 * 1024),
            cost_estimate=pl.CostEstimate(flops=120 * nx * ny * nz, bytes_accessed=16 * nx * ny * nz,
                                          transcendentals=0),
            name="melt_track",
        )(phase, solute, heat_rows, rate_rows, dest_tile, dest_block.reshape(1, rows), active)

    return jax.shard_map(
        on_device,
        mesh=mesh,
        in_specs=(
            P("track", "width", None),
            P("track", "width", None),
            P(("track", "width"), None),
            P(("track", "width"), None),
            P(("track", "width"), None),
            P(("track", "width")),
            P("track", "width"),
        ),
        out_specs=(P("track", "width", None), P("track", "width", None)),
        check_vma=False,
    )
```

```python
import functools

import jax
import jax.numpy as jnp
from jax import lax
from jax.experimental import pallas as pl
from jax.experimental.pallas import tpu as pltpu
from jax.sharding import PartitionSpec as P

BS = 8
CAP = 4
STEPS = 3
KERNEL_MIB = 30
LAST_MIB = 20
LANES = 128
PAD = 8
MESH = pl.DeviceIdType.MESH
HIGH = lax.Precision.HIGHEST

coef_track = 0.9
coef_width = 0.6
coef_depth = 0.35
time_step = 0.1
coupling = 1.6
diffusion = 0.8
center_phase = 1.0 - 2.0 * (coef_track + coef_width + coef_depth)
center_solute = 1.0 - 6.0 * time_step * diffusion


def depth_sum(tiles):
    zt_n = len(tiles)
    lane = lax.broadcasted_iota(jnp.int32, (BS, LANES), 1)
    first_lane = lane == 0
    last_lane = lane == LANES - 1
    up = [pltpu.roll(v, 1, 1) for v in tiles]
    down = [pltpu.roll(v, LANES - 1, 1) for v in tiles]
    sums = []
    for zt in range(zt_n):
        below = jnp.where(first_lane, up[zt - 1] if zt > 0 else 0.0, up[zt])
        above = jnp.where(last_lane, down[zt + 1] if zt < zt_n - 1 else 0.0, down[zt])
        sums.append(below + above)
    return sums

def cell_block(active, theta, src, dst, shift, count, x, by):
    zt_n = src.shape[2]
    x_pad, y_pad = shift
    there = pl.ds(y_pad + BS * by, BS)
    bx = x >> 3
    rate_of = active[bx, by].astype(jnp.float32) * time_step
    here = pl.ds(PAD + BS * by, BS)
    back = pl.ds(PAD + BS * by - 1, BS)
    ahead = pl.ds(PAD + BS * by + 1, BS)
    p = [src[0, x + 1, zt, here, :] for zt in range(zt_n)]
    s = [src[1, x + 1, zt, here, :] for zt in range(zt_n)]
    pz = depth_sum(p)
    sz = depth_sum(s)
    for zt in range(zt_n):
        px = src[0, x, zt, here, :] + src[0, x + 2, zt, here, :]
        py = src[0, x + 1, zt, back, :] + src[0, x + 1, zt, ahead, :]
        sx = src[1, x, zt, here, :] + src[1, x + 2, zt, here, :]
        sy = src[1, x + 1, zt, back, :] + src[1, x + 1, zt, ahead, :]
        square = p[zt] * p[zt]
        bond = 1.0 - square
        drive = coef_track * px + coef_width * py + coef_depth * pz[zt] + p[zt] * (center_phase - square)
        sink = s[zt] if count == 0 else s[zt] + theta[count - 1, bx, zt, by:by + 1, :]
        drive = drive - coupling * bond * bond * sink
        change = rate_of * drive
        dst[0, x + x_pad, zt, there, :] = p[zt] + change
        dst[1, x + x_pad, zt, there, :] = (
            center_solute * s[zt] + (time_step * diffusion) * (sx + sy + sz[zt]) + 0.5 * change)


def sweep(block, xs, bys):
    low_x, high_x, stride = xs

    def body(i, carry):
        for by in bys:
            block(low_x + stride * i, by)
        return carry

    lax.fori_loop(0, (high_x - low_x + stride - 1) // stride, body, 0)


def boundary(block, nx, by_n):
    sweep(block, (0, nx, nx - 1), range(by_n))
    sweep(block, (1, nx - 1, 1), (0, by_n - 1))


def track_kernel(sizes, phase, solute, heat_rows, rate_rows, dest_tile, dest_block, active,
                 f0, f1, theta, y_send, y_recv, label_out, label_in, heat_out, heat_in, rate_out, rate_in,
                 selector,
                 load_sem, x_send_sem, x_recv_sem, y_send_sem, y_recv_sem,
                 label_sems, heat_sems, rate_sems):
    tracks, widths, nx, ny, nz, rows = sizes
    devices = tracks * widths
    zt_n = nz // LANES
    pairs = zt_n // 2
    bx_n = nx // BS
    by_n = ny // BS
    t = lax.axis_index("track")
    w = lax.axis_index("width")
    me = t * widths + w

    def loads():
        out = []
        for f, ref in enumerate((phase, solute)):
            for zt in range(zt_n):
                out.append(pltpu.make_async_copy(
                    ref.at[:, :, pl.ds(zt * LANES, LANES)],
                    f0.at[f, pl.ds(1, nx), zt, pl.ds(PAD, ny), :],
                    load_sem.at[f, zt]))
        return out

    for copy in loads():
        copy.start()

    barrier = pltpu.get_barrier_semaphore()

    def where(k):
        to = lax.rem(me + k, devices)
        return {"track": to // widths, "width": lax.rem(to, widths)}

    def greet(k, carry):
        pl.semaphore_signal(barrier, inc=1, device_id=where(k), device_id_type=MESH)
        return carry

    lax.fori_loop(1, devices, greet, 0)

    trow = dest_tile[...].astype(jnp.float32)
    eye = lax.broadcasted_iota(jnp.int32, (rows, rows), 0) == lax.broadcasted_iota(jnp.int32, (rows, rows), 1)
    tcol = jnp.sum(jnp.where(eye, trow, 0.0), axis=1, keepdims=True)
    before = lax.broadcasted_iota(jnp.int32, (rows, rows), 0) < lax.broadcasted_iota(jnp.int32, (rows, rows), 1)
    rank = jnp.sum(jnp.where(before & (tcol == trow), 1.0, 0.0), axis=0, keepdims=True)
    slot = trow * CAP + rank
    index = lax.broadcasted_iota(jnp.int32, (8 * devices, rows), 0)
    slot_of = ((index >> 3) * CAP + (index & 3)).astype(jnp.float32)
    pick = jnp.where(slot_of == slot, 1.0, 0.0)
    labels = dest_block[...].astype(jnp.float32) + 1.0
    label_col = jnp.sum(pick * labels, axis=1, keepdims=True).reshape(devices, 8, 1)
    diagonal = lax.broadcasted_iota(jnp.int32, (devices, 8, LANES), 1) == lax.broadcasted_iota(
        jnp.int32, (devices, 8, LANES), 2)
    label_out[...] = jnp.sum(jnp.where(diagonal, label_col, 0.0), axis=1, keepdims=True)
    low = lax.broadcasted_iota(jnp.int32, (8 * devices, LANES), 0) & 7 < 4

    def pack_rows(source, target):
        moved = jnp.dot(pick, source[...], precision=HIGH, preferred_element_type=jnp.float32)
        for j in range(pairs):
            first = moved[:, 2 * j * LANES:(2 * j + 1) * LANES]
            second = moved[:, (2 * j + 1) * LANES:(2 * j + 2) * LANES]
            target[:, j] = jnp.where(low, first, second).reshape(devices, 8, LANES)

    pack_rows(heat_rows, heat_out)
    pack_rows(rate_rows, rate_out)

    has = (t > 0, t < tracks - 1, w > 0, w < widths - 1)
    for side in range(2):
        @pl.when(jnp.logical_not(has[side]))
        def _():
            edge = jnp.zeros((2, zt_n, ny, LANES), jnp.float32)
            f0[:, side * (nx + 1), :, pl.ds(PAD, ny), :] = edge
            f1[:, side * (nx + 1), :, pl.ds(PAD, ny), :] = edge

        @pl.when(jnp.logical_not(has[2 + side]))
        def _():
            y_recv[:, side] = jnp.zeros((STEPS, 2, nx, zt_n, 1, LANES), jnp.float32)

    pl.semaphore_wait(barrier, devices - 1)

    def exchange(source, target, sems, k):
        return pltpu.make_async_remote_copy(
            src_ref=source.at[lax.rem(me + k, devices)], dst_ref=target.at[me],
            send_sem=sems.at[0, k], recv_sem=sems.at[1, k],
            device_id=where(k), device_id_type=MESH)

    def own(source, target, sems):
        return pltpu.make_async_copy(source.at[me], target.at[me], sems.at[0, 0])

    def send_all(*triples):
        for triple in triples:
            own(*triple).start()

        def body(k, carry):
            for triple in triples:
                exchange(*triple, k).start()
            return carry

        lax.fori_loop(1, devices, body, 0)

    def wait_all(*triples):
        for triple in triples:
            own(*triple).wait()

        def body(k, carry):
            for triple in triples:
                exchange(*triple, k).wait()
            return carry

        lax.fori_loop(1, devices, body, 0)

    labels_x = (label_out, label_in, label_sems)
    heat_x = (heat_out, heat_in, heat_sems)
    rate_x = (rate_out, rate_in, rate_sems)
    send_all(labels_x, heat_x)

    def x_copy(field, stage, side):
        return pltpu.make_async_remote_copy(
            src_ref=field.at[:, 1 if side == 0 else nx, :, pl.ds(PAD, ny), :],
            dst_ref=field.at[:, nx + 1 if side == 0 else 0, :, pl.ds(PAD, ny), :],
            send_sem=x_send_sem.at[stage, side], recv_sem=x_recv_sem.at[stage, side],
            device_id={"track": t + (2 * side - 1)}, device_id_type=MESH)

    def y_copy(stage, side):
        return pltpu.make_async_remote_copy(
            src_ref=y_send.at[stage, side], dst_ref=y_recv.at[stage, 1 - side],
            send_sem=y_send_sem.at[stage, side], recv_sem=y_recv_sem.at[stage, side],
            device_id={"width": w + (2 * side - 1)}, device_id_type=MESH)

    def send_halo(field, stage):
        for side in range(2):
            @pl.when(has[side])
            def _():
                x_copy(field, stage, side).start()

        def pack(x, carry):
            for side, row in ((0, PAD), (1, PAD + ny - 1)):
                for f in range(2):
                    for zt in range(zt_n):
                        y_send[stage, side, f, x, zt] = field[f, x + 1, zt, pl.ds(row, 1), :]
            return carry

        lax.fori_loop(0, nx, pack, 0)
        for side in range(2):
            @pl.when(has[2 + side])
            def _():
                y_copy(stage, side).start()

    def wait_halo(field, stage):
        for side in range(2):
            @pl.when(has[side])
            def _():
                x_copy(field, stage, side).wait_send()
                x_copy(field, stage, 1 - side).wait_recv()

            @pl.when(has[2 + side])
            def _():
                y_copy(stage, side).wait_send()
                y_copy(stage, 1 - side).wait_recv()

        def unpack(x, carry):
            for side, row in ((0, PAD - 1), (1, PAD + ny)):
                for f in range(2):
                    for zt in range(zt_n):
                        field[f, x + 1, zt, pl.ds(row, 1), :] = y_recv[stage, side, f, x, zt]
            return carry

        lax.fori_loop(0, nx, unpack, 0)

    def heat_block(src, dst, x, by):
        bx = x >> 3
        rate_of = active[bx, by].astype(jnp.float32) * (time_step * coupling)
        here = pl.ds(PAD + BS * by, BS)
        for zt in range(zt_n):
            p = src[0, x + 1, zt, here, :]
            bond = 1.0 - p * p
            change = bond * bond * (rate_of * theta[0, bx, zt, by:by + 1, :])
            dst[0, x + 1, zt, here, :] = dst[0, x + 1, zt, here, :] - change
            dst[1, x + 1, zt, here, :] = dst[1, x + 1, zt, here, :] - 0.5 * change

    inner = range(1, by_n - 1)

    def arrived(rows_in):
        both = jnp.concatenate([rows_in[:, j].reshape(8 * devices, LANES) for j in range(pairs)], axis=1)
        return lax.dot_general(selector[...], both, (((0,), (0,)), ((), ())), precision=HIGH,
                               preferred_element_type=jnp.float32)

    def tile_of(summed, bx, zt):
        at = (zt % 2) * (LANES // 2) + bx * by_n
        return summed[at:at + by_n, (zt // 2) * LANES:(zt // 2 + 1) * LANES]

    for copy in loads():
        copy.wait()
    send_halo(f0, 0)
    send_all(rate_x)

    step0 = functools.partial(cell_block, active, theta, f0, f1, (1, PAD), 0)
    step1 = functools.partial(cell_block, active, theta, f1, f0, (1, PAD), 1)
    step2 = functools.partial(cell_block, active, theta, f0, f1, (1, PAD), 2)
    finish = functools.partial(heat_block, f0, f1)

    sweep(step0, (1, nx - 1, 1), inner)
    wait_halo(f0, 0)
    boundary(step0, nx, by_n)

    wait_all(labels_x, heat_x)
    spread = jnp.where(diagonal, jnp.broadcast_to(label_in[...], (devices, 8, LANES)), 0.0)
    label_in_col = jnp.sum(spread, axis=2, keepdims=True) - 1.0
    place = lax.broadcasted_iota(jnp.int32, (devices, 8, LANES), 2) - (LANES // 2) * (
        lax.broadcasted_iota(jnp.int32, (devices, 8, LANES), 1) >> 2)
    selector[...] = jnp.where(place.astype(jnp.float32) == label_in_col, 1.0, 0.0).reshape(8 * devices, LANES)
    heat = arrived(heat_in)
    for bx in range(bx_n):
        for zt in range(zt_n):
            theta[0, bx, zt] = tile_of(heat, bx, zt)

    boundary(finish, nx, by_n)
    send_halo(f1, 1)
    sweep(finish, (1, nx - 1, 1), inner)

    wait_all(rate_x)
    rate = arrived(rate_in)
    for bx in range(bx_n):
        for zt in range(zt_n):
            whole = theta[0, bx, zt]
            slope = tile_of(rate, bx, zt)
            theta[0, bx, zt] = whole - time_step * slope
            theta[1, bx, zt] = whole - (2 * time_step) * slope

    half = nx // 2
    sweep(step1, (1, half, 1), inner)
    wait_halo(f1, 1)
    boundary(step1, nx, by_n)
    send_halo(f0, 2)
    sweep(step1, (half, nx - 1, 1), inner)
    sweep(step2, (1, half, 1), inner)
    wait_halo(f0, 2)


def last_kernel(active, f0, f1, theta, phase_out, solute_out, late, store_sem):
    zt_n = f0.shape[2]
    nx, ny, _ = phase_out.shape
    by_n = ny // BS
    half = nx // 2

    def stores(part, src, shift, x_at, x_len, y_at, y_len):
        x_pad, y_pad = shift
        out = []
        for f, ref in enumerate((phase_out, solute_out)):
            for zt in range(zt_n):
                out.append(pltpu.make_async_copy(
                    src.at[f, pl.ds(x_pad + x_at, x_len), zt, pl.ds(y_pad + y_at, y_len), :],
                    ref.at[pl.ds(x_at, x_len), pl.ds(y_at, y_len), pl.ds(zt * LANES, LANES)],
                    store_sem.at[part, f, zt]))
        return out

    started = []

    def start(*where):
        copies = stores(len(started) // (2 * zt_n), *where)
        for copy in copies:
            copy.start()
        started.extend(copies)

    start(f1, (1, PAD), 1, half - 1, BS, ny - 2 * BS)
    step = functools.partial(cell_block, active, theta, f0, late, (0, 0), 2)
    ends = (0, by_n - 1)
    sweep(step, (0, half, nx), range(by_n))
    sweep(step, (1, half, 1), ends)
    start(late, (0, 0), 0, 1, 0, ny)
    start(late, (0, 0), 1, half - 1, 0, BS)
    start(late, (0, 0), 1, half - 1, ny - BS, BS)
    pieces = 4
    width = (nx - half) // pieces
    for piece in range(pieces):
        at = half + piece * width
        sweep(step, (at, at + width, 1), range(by_n))
        start(late, (0, 0), at, width, 0, ny)
    for copy in started:
        copy.wait()


def solution(mesh):
    tracks = mesh.shape["track"]
    widths = mesh.shape["width"]
    devices = tracks * widths

    def on_device(phase, solute, heat_rows, rate_rows, dest_tile, dest_block, active):
        nx, ny, nz = phase.shape
        rows = heat_rows.shape[0]
        zt_n = nz // LANES
        pairs = zt_n // 2
        f32 = jnp.float32
        field = pltpu.VMEM((2, nx + 2, zt_n, ny + 2 * PAD, LANES), f32)
        ends = pltpu.VMEM((STEPS, 2, 2, nx, zt_n, 1, LANES), f32)
        label = pltpu.VMEM((devices, 1, LANES), f32)
        moved = pltpu.VMEM((devices, pairs, 8, LANES), f32)
        vmem = pl.BlockSpec(memory_space=pltpu.VMEM)
        any_space = pl.BlockSpec(memory_space=pl.ANY)
        smem = pl.BlockSpec(memory_space=pltpu.SMEM)
        tables = pltpu.VMEM((2, nx // BS, zt_n, ny // BS, LANES), f32)
        f0, f1, theta = pl.pallas_call(
            functools.partial(track_kernel, (tracks, widths, nx, ny, nz, rows)),
            out_shape=(field, field, tables),
            in_specs=[any_space, any_space, vmem, vmem, vmem, vmem, smem],
            out_specs=(vmem, vmem, vmem),
            scratch_shapes=[
                ends, ends, label, label, moved, moved, moved, moved,
                pltpu.VMEM((8 * devices, LANES), f32),
                pltpu.SemaphoreType.DMA((2, zt_n)),
                pltpu.SemaphoreType.DMA((STEPS, 2)),
                pltpu.SemaphoreType.DMA((STEPS, 2)),
                pltpu.SemaphoreType.DMA((STEPS, 2)),
                pltpu.SemaphoreType.DMA((STEPS, 2)),
                pltpu.SemaphoreType.DMA((2, devices)),
                pltpu.SemaphoreType.DMA((2, devices)),
                pltpu.SemaphoreType.DMA((2, devices)),
            ],
            compiler_params=pltpu.CompilerParams(
                collective_id=0, has_side_effects=True, vmem_limit_bytes=KERNEL_MIB * 1024 * 1024),
            cost_estimate=pl.CostEstimate(flops=90 * nx * ny * nz, bytes_accessed=8 * nx * ny * nz,
                                          transcendentals=0),
            name="melt_track",
        )(phase, solute, heat_rows, rate_rows, dest_tile.reshape(1, rows), dest_block.reshape(1, rows), active)
        return pl.pallas_call(
            last_kernel,
            out_shape=(jax.ShapeDtypeStruct(phase.shape, f32), jax.ShapeDtypeStruct(solute.shape, f32)),
            in_specs=[smem, vmem, vmem, vmem],
            out_specs=(any_space, any_space),
            scratch_shapes=[
                pltpu.VMEM((2, nx, zt_n, ny, LANES), f32),
                pltpu.SemaphoreType.DMA((8, 2, zt_n)),
            ],
            compiler_params=pltpu.CompilerParams(vmem_limit_bytes=LAST_MIB * 1024 * 1024),
            cost_estimate=pl.CostEstimate(flops=30 * nx * ny * nz, bytes_accessed=8 * nx * ny * nz,
                                          transcendentals=0),
            name="melt_last",
        )(active, f0, f1, theta)

    return jax.shard_map(
        on_device,
        mesh=mesh,
        in_specs=(
            P("track", "width", None),
            P("track", "width", None),
            P(("track", "width"), None),
            P(("track", "width"), None),
            P(("track", "width"), None),
            P(("track", "width")),
            P("track", "width"),
        ),
        out_specs=(P("track", "width", None), P("track", "width", None)),
        check_vma=False,
    )
```

```python
import functools

import jax
import jax.numpy as jnp
from jax import lax
from jax.experimental import pallas as pl
from jax.experimental.pallas import tpu as pltpu
from jax.sharding import PartitionSpec as P

BS = 8
CAP = 4
STEPS = 3
KERNEL_MIB = 42
LAST_MIB = 20
LANES = 128
PAD = 8
MESH = pl.DeviceIdType.MESH
HIGH = lax.Precision.HIGHEST

coef_track = 0.9
coef_width = 0.6
coef_depth = 0.35
time_step = 0.1
coupling = 1.6
diffusion = 0.8
center_phase = 1.0 - 2.0 * (coef_track + coef_width + coef_depth)
center_solute = 1.0 - 6.0 * time_step * diffusion


def depth_sum(tiles):
    zt_n = len(tiles)
    lane = lax.broadcasted_iota(jnp.int32, (BS, LANES), 1)
    first_lane = lane == 0
    last_lane = lane == LANES - 1
    up = [pltpu.roll(v, 1, 1) for v in tiles]
    down = [pltpu.roll(v, LANES - 1, 1) for v in tiles]
    sums = []
    for zt in range(zt_n):
        below = jnp.where(first_lane, up[zt - 1] if zt > 0 else 0.0, up[zt])
        above = jnp.where(last_lane, down[zt + 1] if zt < zt_n - 1 else 0.0, down[zt])
        sums.append(below + above)
    return sums

def cell_block(active, theta, src, dst, shift, count, x, by):
    zt_n = src.shape[2]
    x_pad, y_pad = shift
    there = pl.ds(y_pad + BS * by, BS)
    bx = x >> 3
    rate_of = active[bx, by].astype(jnp.float32) * time_step
    here = pl.ds(PAD + BS * by, BS)
    back = pl.ds(PAD + BS * by - 1, BS)
    ahead = pl.ds(PAD + BS * by + 1, BS)
    p = [src[0, x + 1, zt, here, :] for zt in range(zt_n)]
    s = [src[1, x + 1, zt, here, :] for zt in range(zt_n)]
    pz = depth_sum(p)
    sz = depth_sum(s)
    for zt in range(zt_n):
        px = src[0, x, zt, here, :] + src[0, x + 2, zt, here, :]
        py = src[0, x + 1, zt, back, :] + src[0, x + 1, zt, ahead, :]
        sx = src[1, x, zt, here, :] + src[1, x + 2, zt, here, :]
        sy = src[1, x + 1, zt, back, :] + src[1, x + 1, zt, ahead, :]
        square = p[zt] * p[zt]
        bond = 1.0 - square
        drive = coef_track * px + coef_width * py + coef_depth * pz[zt] + p[zt] * (center_phase - square)
        sink = s[zt] if count == 0 else s[zt] + theta[count - 1, bx, zt, by:by + 1, :]
        drive = drive - coupling * bond * bond * sink
        change = rate_of * drive
        dst[0, x + x_pad, zt, there, :] = p[zt] + change
        dst[1, x + x_pad, zt, there, :] = (
            center_solute * s[zt] + (time_step * diffusion) * (sx + sy + sz[zt]) + 0.5 * change)


def sweep(block, xs, bys):
    low_x, high_x, stride = xs

    def body(i, carry):
        for by in bys:
            block(low_x + stride * i, by)
        return carry

    lax.fori_loop(0, (high_x - low_x + stride - 1) // stride, body, 0)


def boundary(block, nx, by_n):
    sweep(block, (0, nx, nx - 1), range(by_n))
    sweep(block, (1, nx - 1, 1), (0, by_n - 1))


def track_kernel(sizes, phase, solute, heat_hbm, rate_hbm, tile_hbm, block_hbm, active,
                 f0, f1, theta, y_send, y_recv, label_out, label_in, heat_out, heat_in, rate_out, rate_in,
                 selector, heat_rows, rate_rows, dest_tile, dest_block,
                 load_sem, small_sem, x_send_sem, x_recv_sem, y_send_sem, y_recv_sem,
                 label_sems, heat_sems, rate_sems):
    tracks, widths, nx, ny, nz, rows = sizes
    devices = tracks * widths
    zt_n = nz // LANES
    pairs = zt_n // 2
    bx_n = nx // BS
    by_n = ny // BS
    t = lax.axis_index("track")
    w = lax.axis_index("width")
    me = t * widths + w

    def loads():
        out = []
        for f, ref in enumerate((phase, solute)):
            for zt in range(zt_n):
                out.append(pltpu.make_async_copy(
                    ref.at[:, :, pl.ds(zt * LANES, LANES)],
                    f0.at[f, pl.ds(1, nx), zt, pl.ds(PAD, ny), :],
                    load_sem.at[f, zt]))
        return out

    small = [pltpu.make_async_copy(source, target, small_sem.at[i]) for i, (source, target) in enumerate(
        ((tile_hbm, dest_tile), (block_hbm, dest_block), (heat_hbm, heat_rows), (rate_hbm, rate_rows)))]
    for copy in small:
        copy.start()
    for copy in loads():
        copy.start()

    barrier = pltpu.get_barrier_semaphore()

    def where(k):
        to = lax.rem(me + k, devices)
        return {"track": to // widths, "width": lax.rem(to, widths)}

    def greet(k, carry):
        pl.semaphore_signal(barrier, inc=1, device_id=where(k), device_id_type=MESH)
        return carry

    lax.fori_loop(1, devices, greet, 0)

    for copy in small:
        copy.wait()

    trow = dest_tile[...].astype(jnp.float32)
    eye = lax.broadcasted_iota(jnp.int32, (rows, rows), 0) == lax.broadcasted_iota(jnp.int32, (rows, rows), 1)
    tcol = jnp.sum(jnp.where(eye, trow, 0.0), axis=1, keepdims=True)
    before = lax.broadcasted_iota(jnp.int32, (rows, rows), 0) < lax.broadcasted_iota(jnp.int32, (rows, rows), 1)
    rank = jnp.sum(jnp.where(before & (tcol == trow), 1.0, 0.0), axis=0, keepdims=True)
    slot = trow * CAP + rank
    index = lax.broadcasted_iota(jnp.int32, (8 * devices, rows), 0)
    slot_of = ((index >> 3) * CAP + (index & 3)).astype(jnp.float32)
    pick = jnp.where(slot_of == slot, 1.0, 0.0)
    labels = dest_block[...].astype(jnp.float32) + 1.0
    label_col = jnp.sum(pick * labels, axis=1, keepdims=True).reshape(devices, 8, 1)
    diagonal = lax.broadcasted_iota(jnp.int32, (devices, 8, LANES), 1) == lax.broadcasted_iota(
        jnp.int32, (devices, 8, LANES), 2)
    label_out[...] = jnp.sum(jnp.where(diagonal, label_col, 0.0), axis=1, keepdims=True)
    low = lax.broadcasted_iota(jnp.int32, (8 * devices, LANES), 0) & 7 < 4

    def pack_rows(source, target):
        moved = jnp.dot(pick, source[...], precision=HIGH, preferred_element_type=jnp.float32)
        for j in range(pairs):
            first = moved[:, 2 * j * LANES:(2 * j + 1) * LANES]
            second = moved[:, (2 * j + 1) * LANES:(2 * j + 2) * LANES]
            target[:, j] = jnp.where(low, first, second).reshape(devices, 8, LANES)

    pack_rows(heat_rows, heat_out)

    has = (t > 0, t < tracks - 1, w > 0, w < widths - 1)
    for side in range(2):
        @pl.when(jnp.logical_not(has[side]))
        def _():
            edge = jnp.zeros((2, zt_n, ny, LANES), jnp.float32)
            f0[:, side * (nx + 1), :, pl.ds(PAD, ny), :] = edge
            f1[:, side * (nx + 1), :, pl.ds(PAD, ny), :] = edge

        @pl.when(jnp.logical_not(has[2 + side]))
        def _():
            y_recv[:, side] = jnp.zeros((STEPS, 2, nx, zt_n, 1, LANES), jnp.float32)

    pl.semaphore_wait(barrier, devices - 1)

    def exchange(source, target, sems, k):
        return pltpu.make_async_remote_copy(
            src_ref=source.at[lax.rem(me + k, devices)], dst_ref=target.at[me],
            send_sem=sems.at[0, k], recv_sem=sems.at[1, k],
            device_id=where(k), device_id_type=MESH)

    def own(source, target, sems):
        return pltpu.make_async_copy(source.at[me], target.at[me], sems.at[0, 0])

    def send_all(*triples):
        for triple in triples:
            own(*triple).start()

        def body(k, carry):
            for triple in triples:
                exchange(*triple, k).start()
            return carry

        lax.fori_loop(1, devices, body, 0)

    def wait_all(*triples):
        for triple in triples:
            own(*triple).wait()

        def body(k, carry):
            for triple in triples:
                exchange(*triple, k).wait()
            return carry

        lax.fori_loop(1, devices, body, 0)

    labels_x = (label_out, label_in, label_sems)
    heat_x = (heat_out, heat_in, heat_sems)
    rate_x = (rate_out, rate_in, rate_sems)
    send_all(labels_x, heat_x)

    def x_copy(field, stage, side):
        return pltpu.make_async_remote_copy(
            src_ref=field.at[:, 1 if side == 0 else nx, :, pl.ds(PAD, ny), :],
            dst_ref=field.at[:, nx + 1 if side == 0 else 0, :, pl.ds(PAD, ny), :],
            send_sem=x_send_sem.at[stage, side], recv_sem=x_recv_sem.at[stage, side],
            device_id={"track": t + (2 * side - 1)}, device_id_type=MESH)

    def y_copy(stage, side):
        return pltpu.make_async_remote_copy(
            src_ref=y_send.at[stage, side], dst_ref=y_recv.at[stage, 1 - side],
            send_sem=y_send_sem.at[stage, side], recv_sem=y_recv_sem.at[stage, side],
            device_id={"width": w + (2 * side - 1)}, device_id_type=MESH)

    def send_halo(field, stage):
        for side in range(2):
            @pl.when(has[side])
            def _():
                x_copy(field, stage, side).start()

        def pack(x, carry):
            for side, row in ((0, PAD), (1, PAD + ny - 1)):
                for f in range(2):
                    for zt in range(zt_n):
                        y_send[stage, side, f, x, zt] = field[f, x + 1, zt, pl.ds(row, 1), :]
            return carry

        lax.fori_loop(0, nx, pack, 0, unroll=4)
        for side in range(2):
            @pl.when(has[2 + side])
            def _():
                y_copy(stage, side).start()

    def wait_halo(field, stage):
        for side in range(2):
            @pl.when(has[side])
            def _():
                x_copy(field, stage, side).wait_send()
                x_copy(field, stage, 1 - side).wait_recv()

            @pl.when(has[2 + side])
            def _():
                y_copy(stage, side).wait_send()
                y_copy(stage, 1 - side).wait_recv()

        def unpack(x, carry):
            for side, row in ((0, PAD - 1), (1, PAD + ny)):
                for f in range(2):
                    for zt in range(zt_n):
                        field[f, x + 1, zt, pl.ds(row, 1), :] = y_recv[stage, side, f, x, zt]
            return carry

        lax.fori_loop(0, nx, unpack, 0, unroll=4)

    def heat_block(src, dst, x, by):
        bx = x >> 3
        rate_of = active[bx, by].astype(jnp.float32) * (time_step * coupling)
        here = pl.ds(PAD + BS * by, BS)
        for zt in range(zt_n):
            p = src[0, x + 1, zt, here, :]
            bond = 1.0 - p * p
            change = bond * bond * (rate_of * theta[0, bx, zt, by:by + 1, :])
            dst[0, x + 1, zt, here, :] = dst[0, x + 1, zt, here, :] - change
            dst[1, x + 1, zt, here, :] = dst[1, x + 1, zt, here, :] - 0.5 * change

    inner = range(1, by_n - 1)

    def arrived(rows_in):
        both = jnp.concatenate([rows_in[:, j].reshape(8 * devices, LANES) for j in range(pairs)], axis=1)
        return lax.dot_general(selector[...], both, (((0,), (0,)), ((), ())), precision=HIGH,
                               preferred_element_type=jnp.float32)

    def tile_of(summed, bx, zt):
        at = (zt % 2) * (LANES // 2) + bx * by_n
        return summed[at:at + by_n, (zt // 2) * LANES:(zt // 2 + 1) * LANES]

    for copy in loads():
        copy.wait()
    send_halo(f0, 0)
    pack_rows(rate_rows, rate_out)
    send_all(rate_x)

    step0 = functools.partial(cell_block, active, theta, f0, f1, (1, PAD), 0)
    step1 = functools.partial(cell_block, active, theta, f1, f0, (1, PAD), 1)
    step2 = functools.partial(cell_block, active, theta, f0, f1, (1, PAD), 2)
    finish = functools.partial(heat_block, f0, f1)

    sweep(step0, (1, nx - 1, 1), inner)
    wait_halo(f0, 0)
    boundary(step0, nx, by_n)

    wait_all(labels_x, heat_x)
    spread = jnp.where(diagonal, jnp.broadcast_to(label_in[...], (devices, 8, LANES)), 0.0)
    label_in_col = jnp.sum(spread, axis=2, keepdims=True) - 1.0
    place = lax.broadcasted_iota(jnp.int32, (devices, 8, LANES), 2) - (LANES // 2) * (
        lax.broadcasted_iota(jnp.int32, (devices, 8, LANES), 1) >> 2)
    selector[...] = jnp.where(place.astype(jnp.float32) == label_in_col, 1.0, 0.0).reshape(8 * devices, LANES)
    heat = arrived(heat_in)
    for bx in range(bx_n):
        for zt in range(zt_n):
            theta[0, bx, zt] = tile_of(heat, bx, zt)

    boundary(finish, nx, by_n)
    send_halo(f1, 1)
    sweep(finish, (1, nx - 1, 1), inner)

    wait_all(rate_x)
    rate = arrived(rate_in)
    for bx in range(bx_n):
        for zt in range(zt_n):
            whole = theta[0, bx, zt]
            slope = tile_of(rate, bx, zt)
            theta[0, bx, zt] = whole - time_step * slope
            theta[1, bx, zt] = whole - (2 * time_step) * slope

    half = nx // 2
    sweep(step1, (1, half, 1), inner)
    wait_halo(f1, 1)
    boundary(step1, nx, by_n)
    send_halo(f0, 2)
    sweep(step1, (half, nx - 1, 1), inner)
    sweep(step2, (1, half, 1), inner)
    wait_halo(f0, 2)


def last_kernel(active, f0, f1, theta, phase_out, solute_out, late, store_sem):
    zt_n = f0.shape[2]
    nx, ny, _ = phase_out.shape
    by_n = ny // BS
    half = nx // 2

    def stores(part, src, shift, x_at, x_len, y_at, y_len):
        x_pad, y_pad = shift
        out = []
        for f, ref in enumerate((phase_out, solute_out)):
            for zt in range(zt_n):
                out.append(pltpu.make_async_copy(
                    src.at[f, pl.ds(x_pad + x_at, x_len), zt, pl.ds(y_pad + y_at, y_len), :],
                    ref.at[pl.ds(x_at, x_len), pl.ds(y_at, y_len), pl.ds(zt * LANES, LANES)],
                    store_sem.at[part, f, zt]))
        return out

    started = []

    def start(*where):
        copies = stores(len(started) // (2 * zt_n), *where)
        for copy in copies:
            copy.start()
        started.extend(copies)

    start(f1, (1, PAD), 1, half - 1, BS, ny - 2 * BS)
    step = functools.partial(cell_block, active, theta, f0, late, (0, 0), 2)
    ends = (0, by_n - 1)
    sweep(step, (0, half, nx), range(by_n))
    sweep(step, (1, half, 1), ends)
    start(late, (0, 0), 0, 1, 0, ny)
    start(late, (0, 0), 1, half - 1, 0, BS)
    start(late, (0, 0), 1, half - 1, ny - BS, BS)
    pieces = 4
    width = (nx - half) // pieces
    for piece in range(pieces):
        at = half + piece * width
        sweep(step, (at, at + width, 1), range(by_n))
        start(late, (0, 0), at, width, 0, ny)
    for copy in started:
        copy.wait()


def solution(mesh):
    tracks = mesh.shape["track"]
    widths = mesh.shape["width"]
    devices = tracks * widths

    def on_device(phase, solute, heat_rows, rate_rows, dest_tile, dest_block, active):
        nx, ny, nz = phase.shape
        rows = heat_rows.shape[0]
        zt_n = nz // LANES
        pairs = zt_n // 2
        f32 = jnp.float32
        field = pltpu.VMEM((2, nx + 2, zt_n, ny + 2 * PAD, LANES), f32)
        ends = pltpu.VMEM((STEPS, 2, 2, nx, zt_n, 1, LANES), f32)
        label = pltpu.VMEM((devices, 1, LANES), f32)
        moved = pltpu.VMEM((devices, pairs, 8, LANES), f32)
        vmem = pl.BlockSpec(memory_space=pltpu.VMEM)
        any_space = pl.BlockSpec(memory_space=pl.ANY)
        smem = pl.BlockSpec(memory_space=pltpu.SMEM)
        hbm = pl.BlockSpec(memory_space=pltpu.HBM)
        tables = pltpu.VMEM((2, nx // BS, zt_n, ny // BS, LANES), f32)
        f0, f1, theta = pl.pallas_call(
            functools.partial(track_kernel, (tracks, widths, nx, ny, nz, rows)),
            out_shape=(field, field, tables),
            in_specs=[hbm] * 6 + [smem],
            out_specs=(vmem, vmem, vmem),
            scratch_shapes=[
                ends, ends, label, label, moved, moved, moved, moved,
                pltpu.VMEM((8 * devices, LANES), f32),
                pltpu.VMEM((rows, nz), f32),
                pltpu.VMEM((rows, nz), f32),
                pltpu.VMEM((1, rows), jnp.int32),
                pltpu.VMEM((1, rows), jnp.int32),
                pltpu.SemaphoreType.DMA((2, zt_n)),
                pltpu.SemaphoreType.DMA((4,)),
                pltpu.SemaphoreType.DMA((STEPS, 2)),
                pltpu.SemaphoreType.DMA((STEPS, 2)),
                pltpu.SemaphoreType.DMA((STEPS, 2)),
                pltpu.SemaphoreType.DMA((STEPS, 2)),
                pltpu.SemaphoreType.DMA((2, devices)),
                pltpu.SemaphoreType.DMA((2, devices)),
                pltpu.SemaphoreType.DMA((2, devices)),
            ],
            compiler_params=pltpu.CompilerParams(
                collective_id=0, has_side_effects=True, vmem_limit_bytes=KERNEL_MIB * 1024 * 1024),
            cost_estimate=pl.CostEstimate(flops=90 * nx * ny * nz, bytes_accessed=8 * nx * ny * nz,
                                          transcendentals=0),
            name="melt_track",
        )(phase, solute, heat_rows, rate_rows, dest_tile.reshape(1, rows), dest_block.reshape(1, rows), active)
        return pl.pallas_call(
            last_kernel,
            out_shape=(jax.ShapeDtypeStruct(phase.shape, f32), jax.ShapeDtypeStruct(solute.shape, f32)),
            in_specs=[smem, vmem, vmem, vmem],
            out_specs=(any_space, any_space),
            scratch_shapes=[
                pltpu.VMEM((2, nx, zt_n, ny, LANES), f32),
                pltpu.SemaphoreType.DMA((8, 2, zt_n)),
            ],
            compiler_params=pltpu.CompilerParams(vmem_limit_bytes=LAST_MIB * 1024 * 1024),
            cost_estimate=pl.CostEstimate(flops=30 * nx * ny * nz, bytes_accessed=8 * nx * ny * nz,
                                          transcendentals=0),
            name="melt_last",
        )(active, f0, f1, theta)

    return jax.shard_map(
        on_device,
        mesh=mesh,
        in_specs=(
            P("track", "width", None),
            P("track", "width", None),
            P(("track", "width"), None),
            P(("track", "width"), None),
            P(("track", "width"), None),
            P(("track", "width")),
            P("track", "width"),
        ),
        out_specs=(P("track", "width", None), P("track", "width", None)),
        check_vma=False,
    )
```

```python
import functools

import jax
import jax.numpy as jnp
from jax import lax
from jax.experimental import pallas as pl
from jax.experimental.pallas import tpu as pltpu
from jax.sharding import PartitionSpec as P

BS = 8
CAP = 4
STEPS = 3
KERNEL_MIB = 42
LAST_MIB = 20
LANES = 128
PAD = 8
MESH = pl.DeviceIdType.MESH
HIGH = lax.Precision.HIGHEST

coef_track = 0.9
coef_width = 0.6
coef_depth = 0.35
time_step = 0.1
coupling = 1.6
diffusion = 0.8
center_phase = 1.0 - 2.0 * (coef_track + coef_width + coef_depth)
center_solute = 1.0 - 6.0 * time_step * diffusion


def depth_sum(tiles):
    zt_n = len(tiles)
    lane = lax.broadcasted_iota(jnp.int32, (BS, LANES), 1)
    first_lane = lane == 0
    last_lane = lane == LANES - 1
    up = [pltpu.roll(v, 1, 1) for v in tiles]
    down = [pltpu.roll(v, LANES - 1, 1) for v in tiles]
    sums = []
    for zt in range(zt_n):
        below = jnp.where(first_lane, up[zt - 1] if zt > 0 else 0.0, up[zt])
        above = jnp.where(last_lane, down[zt + 1] if zt < zt_n - 1 else 0.0, down[zt])
        sums.append(below + above)
    return sums

def cell_block(active, theta, src, dst, shift, count, x, by):
    zt_n = src.shape[2]
    x_pad, y_pad = shift
    there = pl.ds(y_pad + BS * by, BS)
    bx = x >> 3
    rate_of = active[bx, by].astype(jnp.float32) * time_step
    here = pl.ds(PAD + BS * by, BS)
    back = pl.ds(PAD + BS * by - 1, BS)
    ahead = pl.ds(PAD + BS * by + 1, BS)
    p = [src[0, x + 1, zt, here, :] for zt in range(zt_n)]
    s = [src[1, x + 1, zt, here, :] for zt in range(zt_n)]
    pz = depth_sum(p)
    sz = depth_sum(s)
    for zt in range(zt_n):
        px = src[0, x, zt, here, :] + src[0, x + 2, zt, here, :]
        py = src[0, x + 1, zt, back, :] + src[0, x + 1, zt, ahead, :]
        sx = src[1, x, zt, here, :] + src[1, x + 2, zt, here, :]
        sy = src[1, x + 1, zt, back, :] + src[1, x + 1, zt, ahead, :]
        square = p[zt] * p[zt]
        bond = 1.0 - square
        drive = coef_track * px + coef_width * py + coef_depth * pz[zt] + p[zt] * (center_phase - square)
        sink = s[zt] if count == 0 else s[zt] + theta[count - 1, bx, zt, by:by + 1, :]
        drive = drive - coupling * bond * bond * sink
        change = rate_of * drive
        dst[0, x + x_pad, zt, there, :] = p[zt] + change
        dst[1, x + x_pad, zt, there, :] = (
            center_solute * s[zt] + (time_step * diffusion) * (sx + sy + sz[zt]) + 0.5 * change)


def sweep(block, xs, bys):
    low_x, high_x, stride = xs

    def body(i, carry):
        for by in bys:
            block(low_x + stride * i, by)
        return carry

    lax.fori_loop(0, (high_x - low_x + stride - 1) // stride, body, 0)


def boundary(block, nx, by_n):
    sweep(block, (0, nx, nx - 1), range(by_n))
    sweep(block, (1, nx - 1, 1), (0, by_n - 1))


def track_kernel(sizes, phase, solute, heat_hbm, rate_hbm, tile_hbm, block_hbm, active,
                 f0, f1, theta, y_send, y_recv, label_out, label_in, heat_out, heat_in, rate_out, rate_in,
                 selector, heat_rows, rate_rows, dest_tile, dest_block,
                 load_sem, small_sem, x_send_sem, x_recv_sem, y_send_sem, y_recv_sem,
                 label_sems, heat_sems, rate_sems):
    tracks, widths, nx, ny, nz, rows = sizes
    devices = tracks * widths
    zt_n = nz // LANES
    pairs = zt_n // 2
    bx_n = nx // BS
    by_n = ny // BS
    t = lax.axis_index("track")
    w = lax.axis_index("width")
    me = t * widths + w

    def loads():
        out = []
        for f, ref in enumerate((phase, solute)):
            for zt in range(zt_n):
                out.append(pltpu.make_async_copy(
                    ref.at[:, :, pl.ds(zt * LANES, LANES)],
                    f0.at[f, pl.ds(1, nx), zt, pl.ds(PAD, ny), :],
                    load_sem.at[f, zt]))
        return out

    small = [pltpu.make_async_copy(source, target, small_sem.at[i]) for i, (source, target) in enumerate(
        ((tile_hbm, dest_tile), (block_hbm, dest_block), (heat_hbm, heat_rows), (rate_hbm, rate_rows)))]
    for copy in small:
        copy.start()
    for copy in loads():
        copy.start()

    barrier = pltpu.get_barrier_semaphore()

    def where(k):
        to = lax.rem(me + k, devices)
        return {"track": to // widths, "width": lax.rem(to, widths)}

    def greet(k, carry):
        pl.semaphore_signal(barrier, inc=1, device_id=where(k), device_id_type=MESH)
        return carry

    lax.fori_loop(1, devices, greet, 0)

    for copy in small:
        copy.wait()

    trow = dest_tile[...].astype(jnp.float32)
    eye = lax.broadcasted_iota(jnp.int32, (rows, rows), 0) == lax.broadcasted_iota(jnp.int32, (rows, rows), 1)
    tcol = jnp.sum(jnp.where(eye, trow, 0.0), axis=1, keepdims=True)
    before = lax.broadcasted_iota(jnp.int32, (rows, rows), 0) < lax.broadcasted_iota(jnp.int32, (rows, rows), 1)
    rank = jnp.sum(jnp.where(before & (tcol == trow), 1.0, 0.0), axis=0, keepdims=True)
    slot = trow * CAP + rank
    index = lax.broadcasted_iota(jnp.int32, (8 * devices, rows), 0)
    slot_of = ((index >> 3) * CAP + (index & 3)).astype(jnp.float32)
    pick = jnp.where(slot_of == slot, 1.0, 0.0)
    labels = dest_block[...].astype(jnp.float32) + 1.0
    label_col = jnp.sum(pick * labels, axis=1, keepdims=True).reshape(devices, 8, 1)
    diagonal = lax.broadcasted_iota(jnp.int32, (devices, 8, LANES), 1) == lax.broadcasted_iota(
        jnp.int32, (devices, 8, LANES), 2)
    label_out[...] = jnp.sum(jnp.where(diagonal, label_col, 0.0), axis=1, keepdims=True)
    low = lax.broadcasted_iota(jnp.int32, (8 * devices, LANES), 0) & 7 < 4

    def pack_rows(source, target):
        moved = jnp.dot(pick, source[...], precision=HIGH, preferred_element_type=jnp.float32)
        for j in range(pairs):
            first = moved[:, 2 * j * LANES:(2 * j + 1) * LANES]
            second = moved[:, (2 * j + 1) * LANES:(2 * j + 2) * LANES]
            target[:, j] = jnp.where(low, first, second).reshape(devices, 8, LANES)

    pack_rows(heat_rows, heat_out)

    has = (t > 0, t < tracks - 1, w > 0, w < widths - 1)
    for side in range(2):
        @pl.when(jnp.logical_not(has[side]))
        def _():
            edge = jnp.zeros((2, zt_n, ny, LANES), jnp.float32)
            f0[:, side * (nx + 1), :, pl.ds(PAD, ny), :] = edge
            f1[:, side * (nx + 1), :, pl.ds(PAD, ny), :] = edge

        @pl.when(jnp.logical_not(has[2 + side]))
        def _():
            y_recv[:, side] = jnp.zeros((STEPS, 2, nx, zt_n, 1, LANES), jnp.float32)

    pl.semaphore_wait(barrier, devices - 1)

    def exchange(source, target, sems, k):
        return pltpu.make_async_remote_copy(
            src_ref=source.at[lax.rem(me + k, devices)], dst_ref=target.at[me],
            send_sem=sems.at[0, k], recv_sem=sems.at[1, k],
            device_id=where(k), device_id_type=MESH)

    def own(source, target, sems):
        return pltpu.make_async_copy(source.at[me], target.at[me], sems.at[0, 0])

    def send_all(*triples):
        for triple in triples:
            own(*triple).start()

        def body(k, carry):
            for triple in triples:
                exchange(*triple, k).start()
            return carry

        lax.fori_loop(1, devices, body, 0)

    def wait_all(*triples):
        for triple in triples:
            own(*triple).wait()

        def body(k, carry):
            for triple in triples:
                exchange(*triple, k).wait()
            return carry

        lax.fori_loop(1, devices, body, 0)

    labels_x = (label_out, label_in, label_sems)
    heat_x = (heat_out, heat_in, heat_sems)
    rate_x = (rate_out, rate_in, rate_sems)
    send_all(labels_x, heat_x)

    def x_copy(field, stage, side):
        return pltpu.make_async_remote_copy(
            src_ref=field.at[:, 1 if side == 0 else nx, :, pl.ds(PAD, ny), :],
            dst_ref=field.at[:, nx + 1 if side == 0 else 0, :, pl.ds(PAD, ny), :],
            send_sem=x_send_sem.at[stage, side], recv_sem=x_recv_sem.at[stage, side],
            device_id={"track": t + (2 * side - 1)}, device_id_type=MESH)

    def y_copy(stage, side):
        return pltpu.make_async_remote_copy(
            src_ref=y_send.at[stage, side], dst_ref=y_recv.at[stage, 1 - side],
            send_sem=y_send_sem.at[stage, side], recv_sem=y_recv_sem.at[stage, side],
            device_id={"width": w + (2 * side - 1)}, device_id_type=MESH)

    def send_halo(field, stage):
        for side in range(2):
            @pl.when(has[side])
            def _():
                x_copy(field, stage, side).start()

        def pack(x, carry):
            for side, row in ((0, PAD), (1, PAD + ny - 1)):
                for f in range(2):
                    for zt in range(zt_n):
                        y_send[stage, side, f, x, zt] = field[f, x + 1, zt, pl.ds(row, 1), :]
            return carry

        lax.fori_loop(0, nx, pack, 0, unroll=4)
        for side in range(2):
            @pl.when(has[2 + side])
            def _():
                y_copy(stage, side).start()

    def wait_halo(field, stage):
        for side in range(2):
            @pl.when(has[side])
            def _():
                x_copy(field, stage, side).wait_send()
                x_copy(field, stage, 1 - side).wait_recv()

            @pl.when(has[2 + side])
            def _():
                y_copy(stage, side).wait_send()
                y_copy(stage, 1 - side).wait_recv()

        def unpack(x, carry):
            for side, row in ((0, PAD - 1), (1, PAD + ny)):
                for f in range(2):
                    for zt in range(zt_n):
                        field[f, x + 1, zt, pl.ds(row, 1), :] = y_recv[stage, side, f, x, zt]
            return carry

        lax.fori_loop(0, nx, unpack, 0, unroll=4)

    def heat_block(src, dst, x, by):
        bx = x >> 3
        rate_of = active[bx, by].astype(jnp.float32) * (time_step * coupling)
        here = pl.ds(PAD + BS * by, BS)
        for zt in range(zt_n):
            p = src[0, x + 1, zt, here, :]
            bond = 1.0 - p * p
            change = bond * bond * (rate_of * theta[0, bx, zt, by:by + 1, :])
            dst[0, x + 1, zt, here, :] = dst[0, x + 1, zt, here, :] - change
            dst[1, x + 1, zt, here, :] = dst[1, x + 1, zt, here, :] - 0.5 * change

    inner = range(1, by_n - 1)

    def arrived(rows_in):
        both = jnp.concatenate([rows_in[:, j].reshape(8 * devices, LANES) for j in range(pairs)], axis=1)
        return lax.dot_general(selector[...], both, (((0,), (0,)), ((), ())), precision=HIGH,
                               preferred_element_type=jnp.float32)

    def tile_of(summed, bx, zt):
        at = (zt % 2) * (LANES // 2) + bx * by_n
        return summed[at:at + by_n, (zt // 2) * LANES:(zt // 2 + 1) * LANES]

    for copy in loads():
        copy.wait()
    send_halo(f0, 0)
    pack_rows(rate_rows, rate_out)
    send_all(rate_x)

    step0 = functools.partial(cell_block, active, theta, f0, f1, (1, PAD), 0)
    step1 = functools.partial(cell_block, active, theta, f1, f0, (1, PAD), 1)
    step2 = functools.partial(cell_block, active, theta, f0, f1, (1, PAD), 2)
    finish = functools.partial(heat_block, f0, f1)

    sweep(step0, (1, nx - 1, 1), inner)
    wait_halo(f0, 0)
    boundary(step0, nx, by_n)

    wait_all(labels_x, heat_x)
    spread = jnp.where(diagonal, jnp.broadcast_to(label_in[...], (devices, 8, LANES)), 0.0)
    label_in_col = jnp.sum(spread, axis=2, keepdims=True) - 1.0
    place = lax.broadcasted_iota(jnp.int32, (devices, 8, LANES), 2) - (LANES // 2) * (
        lax.broadcasted_iota(jnp.int32, (devices, 8, LANES), 1) >> 2)
    selector[...] = jnp.where(place.astype(jnp.float32) == label_in_col, 1.0, 0.0).reshape(8 * devices, LANES)
    heat = arrived(heat_in)
    for bx in range(bx_n):
        for zt in range(zt_n):
            theta[0, bx, zt] = tile_of(heat, bx, zt)

    boundary(finish, nx, by_n)
    send_halo(f1, 1)
    sweep(finish, (1, nx - 1, 1), inner)

    wait_all(rate_x)
    rate = arrived(rate_in)
    for bx in range(bx_n):
        for zt in range(zt_n):
            whole = theta[0, bx, zt]
            slope = tile_of(rate, bx, zt)
            theta[0, bx, zt] = whole - time_step * slope
            theta[1, bx, zt] = whole - (2 * time_step) * slope

    half = nx // 2
    early = nx // 4
    sweep(step1, (1, early, 1), inner)
    wait_halo(f1, 1)
    boundary(step1, nx, by_n)
    send_halo(f0, 2)
    sweep(step1, (early, nx - 1, 1), inner)
    sweep(step2, (1, half, 1), inner)
    wait_halo(f0, 2)


def last_kernel(active, f0, f1, theta, phase_out, solute_out, late, store_sem):
    zt_n = f0.shape[2]
    nx, ny, _ = phase_out.shape
    by_n = ny // BS
    half = nx // 2

    def stores(part, src, shift, x_at, x_len, y_at, y_len):
        x_pad, y_pad = shift
        out = []
        for f, ref in enumerate((phase_out, solute_out)):
            for zt in range(zt_n):
                out.append(pltpu.make_async_copy(
                    src.at[f, pl.ds(x_pad + x_at, x_len), zt, pl.ds(y_pad + y_at, y_len), :],
                    ref.at[pl.ds(x_at, x_len), pl.ds(y_at, y_len), pl.ds(zt * LANES, LANES)],
                    store_sem.at[part, f, zt]))
        return out

    started = []

    def start(*where):
        copies = stores(len(started) // (2 * zt_n), *where)
        for copy in copies:
            copy.start()
        started.extend(copies)

    start(f1, (1, PAD), 1, half - 1, BS, ny - 2 * BS)
    step = functools.partial(cell_block, active, theta, f0, late, (0, 0), 2)
    ends = (0, by_n - 1)
    sweep(step, (0, half, nx), range(by_n))
    sweep(step, (1, half, 1), ends)
    start(late, (0, 0), 0, 1, 0, ny)
    start(late, (0, 0), 1, half - 1, 0, BS)
    start(late, (0, 0), 1, half - 1, ny - BS, BS)
    pieces = 4
    width = (nx - half) // pieces
    for piece in range(pieces):
        at = half + piece * width
        sweep(step, (at, at + width, 1), range(by_n))
        start(late, (0, 0), at, width, 0, ny)
    for copy in started:
        copy.wait()


def solution(mesh):
    tracks = mesh.shape["track"]
    widths = mesh.shape["width"]
    devices = tracks * widths

    def on_device(phase, solute, heat_rows, rate_rows, dest_tile, dest_block, active):
        nx, ny, nz = phase.shape
        rows = heat_rows.shape[0]
        zt_n = nz // LANES
        pairs = zt_n // 2
        f32 = jnp.float32
        field = pltpu.VMEM((2, nx + 2, zt_n, ny + 2 * PAD, LANES), f32)
        ends = pltpu.VMEM((STEPS, 2, 2, nx, zt_n, 1, LANES), f32)
        label = pltpu.VMEM((devices, 1, LANES), f32)
        moved = pltpu.VMEM((devices, pairs, 8, LANES), f32)
        vmem = pl.BlockSpec(memory_space=pltpu.VMEM)
        any_space = pl.BlockSpec(memory_space=pl.ANY)
        smem = pl.BlockSpec(memory_space=pltpu.SMEM)
        hbm = pl.BlockSpec(memory_space=pltpu.HBM)
        tables = pltpu.VMEM((2, nx // BS, zt_n, ny // BS, LANES), f32)
        f0, f1, theta = pl.pallas_call(
            functools.partial(track_kernel, (tracks, widths, nx, ny, nz, rows)),
            out_shape=(field, field, tables),
            in_specs=[hbm] * 6 + [smem],
            out_specs=(vmem, vmem, vmem),
            scratch_shapes=[
                ends, ends, label, label, moved, moved, moved, moved,
                pltpu.VMEM((8 * devices, LANES), f32),
                pltpu.VMEM((rows, nz), f32),
                pltpu.VMEM((rows, nz), f32),
                pltpu.VMEM((1, rows), jnp.int32),
                pltpu.VMEM((1, rows), jnp.int32),
                pltpu.SemaphoreType.DMA((2, zt_n)),
                pltpu.SemaphoreType.DMA((4,)),
                pltpu.SemaphoreType.DMA((STEPS, 2)),
                pltpu.SemaphoreType.DMA((STEPS, 2)),
                pltpu.SemaphoreType.DMA((STEPS, 2)),
                pltpu.SemaphoreType.DMA((STEPS, 2)),
                pltpu.SemaphoreType.DMA((2, devices)),
                pltpu.SemaphoreType.DMA((2, devices)),
                pltpu.SemaphoreType.DMA((2, devices)),
            ],
            compiler_params=pltpu.CompilerParams(
                collective_id=0, has_side_effects=True, vmem_limit_bytes=KERNEL_MIB * 1024 * 1024),
            cost_estimate=pl.CostEstimate(flops=90 * nx * ny * nz, bytes_accessed=8 * nx * ny * nz,
                                          transcendentals=0),
            name="melt_track",
        )(phase, solute, heat_rows, rate_rows, dest_tile.reshape(1, rows), dest_block.reshape(1, rows), active)
        return pl.pallas_call(
            last_kernel,
            out_shape=(jax.ShapeDtypeStruct(phase.shape, f32), jax.ShapeDtypeStruct(solute.shape, f32)),
            in_specs=[smem, vmem, vmem, vmem],
            out_specs=(any_space, any_space),
            scratch_shapes=[
                pltpu.VMEM((2, nx, zt_n, ny, LANES), f32),
                pltpu.SemaphoreType.DMA((8, 2, zt_n)),
            ],
            compiler_params=pltpu.CompilerParams(vmem_limit_bytes=LAST_MIB * 1024 * 1024),
            cost_estimate=pl.CostEstimate(flops=30 * nx * ny * nz, bytes_accessed=8 * nx * ny * nz,
                                          transcendentals=0),
            name="melt_last",
        )(active, f0, f1, theta)

    return jax.shard_map(
        on_device,
        mesh=mesh,
        in_specs=(
            P("track", "width", None),
            P("track", "width", None),
            P(("track", "width"), None),
            P(("track", "width"), None),
            P(("track", "width"), None),
            P(("track", "width")),
            P("track", "width"),
        ),
        out_specs=(P("track", "width", None), P("track", "width", None)),
        check_vma=False,
    )
```
